32 devices in a mesh: dp: 2 (over x), mp: 16 (over z, y, core).
Axes of the slice: x: 2, y: 2, z: 4, core: 2. Of those that a mesh axis runs over, the one named last changes fastest.
Arguments:
- tokens: bfloat16 [512, 2048], P('dp'), may hold values from -6 to 6
- domain_ids: int32 [512], P('dp'), may hold values from 0 to 21
- domain_bias: bfloat16 [22, 2048], replicated, may hold values from -3 to 3
- dense_gate: bfloat16 [2048, 10944], P(None, 'mp'), may hold values from -0.125 to 0.125
- dense_up: bfloat16 [2048, 10944], P(None, 'mp'), may hold values from -0.125 to 0.125
- dense_down: bfloat16 [10944, 2048], P('mp'), may hold values from -0.0546875 to 0.0546875
- shared_gate: bfloat16 [2048, 2816], P(None, 'mp'), may hold values from -0.125 to 0.125
- shared_up: bfloat16 [2048, 2816], P(None, 'mp'), may hold values from -0.125 to 0.125
- shared_down: bfloat16 [2816, 2048], P('mp'), may hold values from -0.109375 to 0.109375
- expert_gate: bfloat16 [16, 2048, 1408], P('mp', None, 'dp'), may hold values from -0.125 to 0.125
- expert_up: bfloat16 [16, 2048, 1408], P('mp', None, 'dp'), may hold values from -0.125 to 0.125
- expert_down: bfloat16 [16, 1408, 2048], P('mp', 'dp'), may hold values from -0.15625 to 0.15625
- expert_ids: int32 [512, 6], P('dp'), may hold values from 0 to 15, all different within a row; in each aligned block of 16 rows (0 to 15, 16 to 31, ...) at most 12 rows name the same one
- route_weights: float32 [512, 6], P('dp'), may hold values from 0.05 to 0.6
Outputs:
- mixed: bfloat16 [512, 2048], P(('dp', 'mp'))
The draws below stay inside these ranges and needn't reach their ends.
Inputs may be any that keep to these rules, and one draw needn't show every extreme that they name: `expert_ids`: each row names 6 different experts; in the 16 rows of one device (aligned blocks in order) no expert is named more than 12 times, and in some blocks one expert exactly 12 times.
All inputs are finite; a program needn't handle non-finite values.
Results may differ from the reference program's by a relative error of at most 0.009.
Values may be sent and summed in bfloat16 or wider, within the bound.
A program may use at most 128 MiB of HBM per device.

```python
import math
import jax
import jax.numpy as jnp
import numpy as np
from jax import lax

D = 2048
FF = 10944
SH = 2816
EH = 1408
TOP = 6
DOMAINS = 22
TOK_DEV = 16
EXPERTS = 16
TOKENS = 512
MOST = 12
N_DP = 2
N_MP = 16


def set_ends(array, rng, least, high):
    longest = array.shape.index(max(array.shape))
    spots = []
    for shift in (0, 1):
        where = [jax.random.randint(jax.random.fold_in(rng, axis), (), 0, length) for axis, length in enumerate(array.shape)]
        where[longest] = (where[longest] + shift) % array.shape[longest]
        spots.append(tuple(where))
    return array.at[spots[0]].set(least).at[spots[1]].set(high)


def block_levels(stream_key, dims, split, least, top_value):
    gain, own = 1.0, jax.random.fold_in(stream_key, 6)
    for dim, blocks in split:
        heights = jnp.exp(jax.random.uniform(jax.random.fold_in(own, dim), (blocks,), jnp.float32, least / len(split), top_value / len(split)))
        gain = gain * jnp.repeat(heights, dims[dim] // blocks).reshape([-1 if axis == dim else 1 for axis in range(len(dims))])
    return gain


def rank_bounds(number_of, skew):
    portions = [(1 << 20) // math.isqrt(grade ** skew) + 1 for grade in range(1, number_of + 1)]
    width = 1 + sum(portions) // (1 << 30)
    return np.cumsum(np.array([max(1, weight // width) for weight in portions]))


def ranked_ids(stream_key, dims, count, skew):
    table = rank_bounds(count, skew)
    pick = jax.random.randint(jax.random.fold_in(stream_key, 1), dims, 0, int(table[count - 1]))
    standing = jnp.searchsorted(jnp.asarray(table, jnp.int32), pick, side="right")
    return jax.random.permutation(jax.random.fold_in(stream_key, 2), count)[standing].astype(jnp.int32)


def deal_out(key, own, number, rows, amount, top, limit, lean):
    ranking = jax.random.permutation(key, amount)
    crowded, ordinary = portions_of(amount, rows * top, limit, lean, True), portions_of(amount, rows * top, limit, lean, False)
    places = jnp.arange(amount)

    def named(sizes, rotation):
        used = int((sizes > 0).sum())
        fixed = max(1, used // 4)
        passed = fixed + (places - fixed + rotation * (used - fixed)) % max(1, amount - fixed)
        return jnp.zeros((amount,), jnp.int32).at[ranking[jnp.where(places < fixed, places, passed)]].set(jnp.asarray(sizes, jnp.int32))

    sizes = jnp.where(number % 4 == 0, named(crowded, number // 4), named(ordinary, number - number // 4 - 1))
    mixed = jax.random.permutation(jax.random.fold_in(own, 3), amount)
    source_of, receiver = mixed[0:amount // 2 * 2:2], mixed[1:amount // 2 * 2:2]
    room = jnp.minimum(sizes[source_of] - 1, limit - sizes[receiver]) // 2
    room = jnp.where((source_of == ranking[0]) | (receiver == ranking[0]) | (sizes[receiver] == 0), 0, jnp.maximum(room, 0))
    passed = jax.random.randint(jax.random.fold_in(own, 4), (amount // 2,), 0, 1 << 20) % (room + 1)
    sizes = sizes.at[source_of].add(-passed).at[receiver].add(passed)
    items = jnp.searchsorted(jnp.cumsum(sizes), jnp.arange(rows * top), side="right").astype(jnp.int32)
    listing = items.reshape(top, rows).T
    listing = listing[jax.random.permutation(jax.random.fold_in(own, 1), rows)]
    rotation = jax.random.randint(jax.random.fold_in(own, 2), (rows, 1), 0, top)
    return jnp.take_along_axis(listing, (jnp.arange(top)[None, :] + rotation) % top, axis=1)


def portions_of(number_of, total, most, lean, full):
    weights = [(1 << 20) // math.isqrt(rank ** lean) + 1 for rank in range(1, number_of + 1)]
    largest = most if full else min(most, max(-(-total // number_of), total * weights[0] // sum(weights)))
    least = 1 if total - largest >= number_of - 1 else 0
    given, spare = [largest] + [least] * (number_of - 1), total - largest - least * (number_of - 1)
    while spare > 0:
        free = [i for i in range(1, number_of) if given[i] < largest] or [i for i in range(1, number_of) if given[i] < most]
        mass, left = sum([weights[i] for i in free]), spare
        for i in free:
            more = min(most - given[i], max(1, left * weights[i] // mass), spare)
            given[i] = given[i] + more
            spare = spare - more
    return np.array(given)


def normal_values(rng, dims, width, reach, pieces=(), held_as=jnp.bfloat16):
    drawn = jax.random.normal(rng, dims, jnp.float32) * width
    if len(pieces) > 0:
        drawn = block_levels(rng, dims, pieces, -0.22, 0.18) * drawn
    return jnp.clip(drawn, min=-reach, max=reach).astype(held_as)


def setup_inputs(seed: int = 0) -> dict:
    key_of = jax.random.split(jax.random.key(seed), 15)
    tokens = normal_values(key_of[0], (TOKENS, D), 1.0, 6.0, ((0, 2),))
    domain_ids = set_ends(ranked_ids(key_of[1], (TOKENS,), DOMAINS, 2), jax.random.fold_in(key_of[1], 3), 0, DOMAINS - 1).astype(jnp.int32)
    domain_bias = normal_values(key_of[2], (DOMAINS, D), 0.5, 3.0)
    dense_gate = normal_values(key_of[3], (D, FF), D ** -0.5, 0.125, ((1, 16),))
    dense_up = normal_values(key_of[4], (D, FF), D ** -0.5, 0.125, ((1, 16),))
    dense_down = normal_values(key_of[5], (FF, D), FF ** -0.5, 0.0546875, ((0, 16),))
    shared_gate = normal_values(key_of[6], (D, SH), D ** -0.5, 0.125, ((1, 16),))
    shared_up = normal_values(key_of[7], (D, SH), D ** -0.5, 0.125, ((1, 16),))
    shared_down = normal_values(key_of[8], (SH, D), SH ** -0.5, 0.109375, ((0, 16),))
    expert_gate = normal_values(key_of[9], (EXPERTS, D, EH), D ** -0.5, 0.125, ((0, 16), (2, 2)))
    expert_up = normal_values(key_of[10], (EXPERTS, D, EH), D ** -0.5, 0.125, ((0, 16), (2, 2)))
    expert_down = normal_values(key_of[11], (EXPERTS, EH, D), EH ** -0.5, 0.15625, ((0, 16), (1, 2)))
    expert_ids_keys = jax.random.split(jax.random.fold_in(key_of[12], 1), TOKENS // TOK_DEV)
    expert_ids_turns = jax.random.permutation(jax.random.fold_in(key_of[12], 3), TOKENS // TOK_DEV)
    expert_ids = jax.vmap(lambda own, number: deal_out(jax.random.fold_in(key_of[12], 2), own, number, TOK_DEV, EXPERTS, TOP, MOST, 2))(expert_ids_keys, expert_ids_turns).reshape((TOKENS, TOP))
    route_weights = jnp.clip(jnp.exp(math.log(0.6) - 2.4849067 * jax.random.uniform(key_of[13], (TOKENS, TOP), jnp.float32) ** block_levels(key_of[13], (TOKENS, TOP), ((0, 2),), -0.2, 0.2)), 0.05, 0.6)
    return dict(tokens=tokens, domain_ids=domain_ids, domain_bias=domain_bias, dense_gate=dense_gate, dense_up=dense_up, dense_down=dense_down, shared_gate=shared_gate, shared_up=shared_up, shared_down=shared_down, expert_gate=expert_gate, expert_up=expert_up, expert_down=expert_down, expert_ids=expert_ids, route_weights=route_weights)


def swiglu(rows, w_gate, w_up):
    gate = jnp.dot(rows, w_gate, preferred_element_type=jnp.float32)
    up = jnp.dot(rows, w_up, preferred_element_type=jnp.float32)
    return (jax.nn.silu(gate) * up).astype(jnp.bfloat16)


def reference(tokens, domain_ids, domain_bias, dense_gate, dense_up, dense_down, shared_gate, shared_up, shared_down, expert_gate, expert_up, expert_down, expert_ids, route_weights):
    stream = (tokens.astype(jnp.float32) + domain_bias.astype(jnp.float32)[domain_ids]).astype(jnp.bfloat16)
    dense_hidden = swiglu(stream, dense_gate, dense_up)
    resid = (stream.astype(jnp.float32) + jnp.dot(dense_hidden, dense_down, preferred_element_type=jnp.float32)).astype(jnp.bfloat16)
    shared_hidden = swiglu(resid, shared_gate, shared_up)
    shared_out = jnp.dot(shared_hidden, shared_down, preferred_element_type=jnp.float32)
    capacity = N_DP * N_MP * MOST

    def one_expert(carry, inputs):
        expert, w_gate, w_up, w_down = inputs
        hit = expert_ids == expert
        chosen = jnp.any(hit, axis=1)
        weight = jnp.sum(jnp.where(hit, route_weights, 0.0), axis=1)
        order = jnp.argsort(jnp.where(chosen, 0, 1).astype(jnp.int32), stable=True)[:capacity].astype(jnp.int32)
        hidden = swiglu(resid[order], w_gate, w_up)
        outputs = jnp.dot(hidden, w_down, preferred_element_type=jnp.float32).astype(jnp.bfloat16)
        coef = jnp.where(chosen[order], weight[order], 0.0)
        carry = carry.at[order].add(coef[:, None] * outputs.astype(jnp.float32))
        return carry, None

    start = jnp.zeros(resid.shape, jnp.float32)
    experts = jnp.arange(expert_gate.shape[0], dtype=jnp.int32)
    routed, _ = lax.scan(one_expert, start, (experts, expert_gate, expert_up, expert_down))
    return (resid.astype(jnp.float32) + shared_out + routed).astype(jnp.bfloat16)
```

```python
import functools

import jax
import jax.numpy as jnp
from jax import lax
from jax.experimental import pallas as pl
from jax.experimental.pallas import tpu as pltpu
from jax.sharding import PartitionSpec as P

F32 = jnp.float32
BF16 = jnp.bfloat16
CORES = 2
CHUNKS = 4
ROW_TILE = 256
COL_TILE = 256


def dot(a, b):
    return jnp.dot(a, b, preferred_element_type=F32)


def kernel(
    n_dp,
    n_mp,
    tokens,
    domain_ids,
    domain_bias,
    dense_gate,
    dense_up,
    dense_down,
    shared_gate,
    shared_up,
    shared_down,
    expert_gate,
    expert_up,
    expert_down,
    expert_ids,
    route_weights,
    out,
    stream,
    wdg,
    wdu,
    wdd,
    wsg,
    wsu,
    wsd,
    weg,
    weu,
    wed,
    dense_hid,
    shared_hid,
    expert_hid,
    coef,
    part,
    resid,
    pair1,
    plane1,
    pair2,
    cross,
    plane2,
    load_sem,
    coef_ss,
    coef_rs,
    pair1_ss,
    pair1_rs,
    plane1_ss,
    plane1_rs,
    ring_ss,
    ring_rs,
    sib_ss,
    sib_rs,
    dup_ss,
    dup_rs,
    pair2_ss,
    pair2_rs,
    cross_ss,
    cross_rs,
    plane2_ss,
    plane2_rs,
):
    group = lax.axis_index("dp")
    column = lax.axis_index("mp")
    chip = column // CORES
    core = lax.rem(column, CORES)
    other = 1 - core
    chips = n_mp // CORES
    rows, width = stream.shape
    block = rows // n_mp
    tile = min(rows, ROW_TILE)
    tiles = rows // tile
    tile_chips = tile // (CORES * block)
    cols = width // CHUNKS
    sibling = (group, chip * CORES + other)

    def chip_at(j):
        return lax.rem(chip + j, chips)

    def chip_from(j):
        return lax.rem(chip + (chips - j), chips)

    def group_at(i):
        return lax.rem(group + i, n_dp)

    def group_from(i):
        return lax.rem(group + (n_dp - i), n_dp)

    def peer(j):
        return (group, chip_at(j) * CORES + core)

    def partner(i):
        return (group_at(i), column)

    def remote(src, dst, ss, rs, device):
        return pltpu.make_async_remote_copy(
            src_ref=src,
            dst_ref=dst,
            send_sem=ss,
            recv_sem=rs,
            device_id=device,
            device_id_type=pl.DeviceIdType.MESH,
        )

    def each_tile(fn):
        if tiles == 1:
            fn(0)
        else:
            pl.loop(0, tiles)(fn)

    def row_span(t):
        return pl.ds(t * tile, tile) if tiles == 1 else pl.ds(pl.multiple_of(t * tile, tile), tile)

    def chip_span(t):
        return pl.ds(t * tile_chips, tile_chips)

    loads = []
    for index, (src, dst) in enumerate(
        (
            (tokens, stream),
            (dense_gate, wdg),
            (dense_up, wdu),
            (dense_down, wdd),
            (shared_gate, wsg),
            (shared_up, wsu),
            (shared_down, wsd),
            (expert_gate.at[0], weg),
            (expert_up.at[0], weu),
            (expert_down.at[0], wed),
        )
    ):
        load = pltpu.make_async_copy(src, dst, load_sem.at[index])
        load.start()
        loads.append(load)

    barrier = pltpu.get_barrier_semaphore()
    contacts = [sibling]
    contacts += [peer(j) for j in range(1, chips)]
    contacts += [partner(i) for i in range(1, n_dp)]
    for device in contacts:
        pl.semaphore_signal(barrier, inc=1, device_id=device, device_id_type=pl.DeviceIdType.MESH)

    named = expert_ids[...] == column
    own_coef = jnp.sum(jnp.where(named, route_weights[...], 0.0), axis=1, keepdims=True)
    coef[group] = jnp.broadcast_to(own_coef, coef.shape[1:])

    loads[0].wait()

    domains = domain_bias.shape[0]

    def add_bias(t):
        span = row_span(t)
        numbers = lax.broadcasted_iota(jnp.int32, (tile, domains), 1)
        lookup = jnp.where(domain_ids[span, :] == numbers, 1.0, 0.0).astype(BF16)
        stream[span, :] = (
            stream[span, :].astype(F32) + dot(lookup, domain_bias[...])
        ).astype(BF16)

    each_tile(add_bias)

    def swiglu(read, w_gate, w_up, hidden):
        units = w_gate.shape[1]

        def one(t):
            span = row_span(t)
            x = read(t)
            for start in range(0, units, COL_TILE):
                stop = min(units, start + COL_TILE)
                gate = dot(x, w_gate[:, start:stop])
                up = dot(x, w_up[:, start:stop])
                hidden[span, start:stop] = (gate / (1.0 + jnp.exp(-gate)) * up).astype(BF16)

        each_tile(one)

    loads[1].wait()
    loads[2].wait()
    swiglu(lambda t: stream[row_span(t), :], wdg, wdu, dense_hid)

    pl.semaphore_wait(barrier, len(contacts))
    coef_sends = [
        remote(coef.at[group], coef.at[group], coef_ss.at[i - 1], coef_rs.at[i - 1], partner(i))
        for i in range(1, n_dp)
    ]
    for copy in coef_sends:
        copy.start()

    loads[3].wait()
    pair_sends = []
    for h in range(CHUNKS):
        span = slice(h * cols, (h + 1) * cols)

        def down(t):
            value = dot(dense_hid[row_span(t), :], wdd[:, span])
            part[chip_span(t), :, :, span] = value.astype(BF16).reshape(
                tile_chips, CORES, block, cols
            )

        each_tile(down)
        copy = remote(
            part.at[:, other, :, span],
            pair1.at[:, :, span],
            pair1_ss.at[h],
            pair1_rs.at[h],
            sibling,
        )
        copy.start()
        pair_sends.append(copy)
    for copy in pair_sends:
        copy.wait_recv()
    plane_sends = []
    for j in range(1, chips):
        k = chip_at(j)
        part[k, core] = (part[k, core].astype(F32) + pair1[k].astype(F32)).astype(BF16)
        copy = remote(
            part.at[k, core], plane1.at[j], plane1_ss.at[j], plane1_rs.at[j], peer(j)
        )
        copy.start()
        plane_sends.append(copy)
    own_rows = pl.ds(pl.multiple_of(column * block, block), block)
    total = part[chip, core].astype(F32) + pair1[chip].astype(F32)
    for j in range(1, chips):
        plane_sends[j - 1].wait_recv()
        total = total + plane1[j].astype(F32)
    resid[group, chip, core] = (stream[own_rows, :].astype(F32) + total).astype(BF16)

    ring_sends, sib_sends, dup_sends = [], [], []

    def spread(j):
        k = chip_from(j)
        mine = resid.at[group, k, core]
        for i in range(1, n_dp):
            copy = remote(mine, mine, dup_ss.at[i - 1, j], dup_rs.at[i - 1, j], partner(i))
            copy.start()
            dup_sends.append(copy)
        copy = remote(mine, mine, sib_ss.at[0, j], sib_rs.at[0, j], sibling)
        copy.start()
        sib_sends.append(copy)

    own = resid.at[group, chip, core]
    for j in range(1, chips):
        copy = remote(own, own, ring_ss.at[j], ring_rs.at[j], peer(j))
        copy.start()
        ring_sends.append(copy)
    spread(0)
    for j in range(1, chips):
        landed = resid.at[group, chip_from(j), core]
        remote(landed, landed, ring_ss.at[j], ring_rs.at[j], peer(j)).wait_recv()
        spread(j)

    def from_sibling(i):
        for j in range(chips):
            landed = resid.at[group_from(i), chip_from(j), other]
            remote(landed, landed, sib_ss.at[i, j], sib_rs.at[i, j], sibling).wait_recv()

    def group_rows(g):
        return lambda t: resid[g, chip_span(t)].reshape(tile, width)

    from_sibling(0)
    for index in (4, 5, 7, 8):
        loads[index].wait()
    swiglu(group_rows(group), wsg, wsu, shared_hid)
    for i in range(1, n_dp):
        for j in range(chips):
            landed = resid.at[group_from(i), chip_from(j), core]
            remote(
                landed, landed, dup_ss.at[i - 1, j], dup_rs.at[i - 1, j], partner(i)
            ).wait_recv()
            copy = remote(landed, landed, sib_ss.at[i, j], sib_rs.at[i, j], sibling)
            copy.start()
            sib_sends.append(copy)
    for copy in coef_sends:
        copy.wait()
    loads[6].wait()
    loads[9].wait()
    for copy in pair_sends + plane_sends + ring_sends + dup_sends:
        copy.wait_send()

    cross_sends, pair2_sends = [], []
    for i in range(1, n_dp):
        from_sibling(i)
    for copy in sib_sends:
        copy.wait_send()
    for i in range(1, n_dp):
        g = group_from(i)
        swiglu(group_rows(g), weg, weu, expert_hid)
        sends = []
        for h in range(CHUNKS):
            span = slice(h * cols, (h + 1) * cols)

            def down_other(t):
                value = coef[g, row_span(t), 0:1] * dot(expert_hid[row_span(t), :], wed[:, span])
                resid[g, chip_span(t), :, :, span] = value.astype(BF16).reshape(
                    tile_chips, CORES, block, cols
                )

            each_tile(down_other)
            copy = remote(
                resid.at[g, :, other, :, span],
                pair2.at[i, :, :, span],
                pair2_ss.at[i, h],
                pair2_rs.at[i, h],
                sibling,
            )
            copy.start()
            sends.append(copy)
        for copy in sends:
            copy.wait_recv()
        pair2_sends += sends
        for j in range(chips):
            k = chip_at(j)
            resid[g, k, core] = (
                resid[g, k, core].astype(F32) + pair2[i, k].astype(F32)
            ).astype(BF16)
            copy = remote(
                resid.at[g, k, core],
                cross.at[i - 1, k],
                cross_ss.at[i - 1, j],
                cross_rs.at[i - 1, j],
                (g, column),
            )
            copy.start()
            cross_sends.append(copy)

    swiglu(group_rows(group), weg, weu, expert_hid)
    sends = []
    for h in range(CHUNKS):
        span = slice(h * cols, (h + 1) * cols)

        def down_own(t):
            value = dot(shared_hid[row_span(t), :], wsd[:, span])
            value = value + coef[group, row_span(t), 0:1] * dot(
                expert_hid[row_span(t), :], wed[:, span]
            )
            part[chip_span(t), :, :, span] = value.astype(BF16).reshape(
                tile_chips, CORES, block, cols
            )

        each_tile(down_own)
        copy = remote(
            part.at[:, other, :, span],
            pair2.at[0, :, :, span],
            pair2_ss.at[0, h],
            pair2_rs.at[0, h],
            sibling,
        )
        copy.start()
        sends.append(copy)
    for copy in sends:
        copy.wait_recv()
    pair2_sends += sends
    plane_sends = []
    total = None
    for j in list(range(1, chips)) + [0]:
        k = chip_at(j)
        value = part[k, core].astype(F32) + pair2[0, k].astype(F32)
        for i in range(1, n_dp):
            landed = cross.at[i - 1, k]
            remote(
                landed, landed, cross_ss.at[i - 1, j], cross_rs.at[i - 1, j], partner(i)
            ).wait_recv()
            value = value + cross[i - 1, k].astype(F32)
        if j == 0:
            total = value
            continue
        part[k, core] = value.astype(BF16)
        copy = remote(
            part.at[k, core], plane2.at[j], plane2_ss.at[j], plane2_rs.at[j], peer(j)
        )
        copy.start()
        plane_sends.append(copy)
    total = total + resid[group, chip, core].astype(F32)
    for j in range(1, chips):
        plane_sends[j - 1].wait_recv()
        total = total + plane2[j].astype(F32)
    out[...] = total.astype(BF16)
    for copy in plane_sends + pair2_sends + cross_sends:
        copy.wait_send()


def body(n_dp, n_mp, *args):
    (
        tokens,
        domain_ids,
        domain_bias,
        dense_gate,
        dense_up,
        dense_down,
        shared_gate,
        shared_up,
        shared_down,
        expert_gate,
        expert_up,
        expert_down,
        expert_ids,
        route_weights,
    ) = args
    rows, width = tokens.shape
    block = rows // n_mp
    chips = n_mp // CORES
    ff, sh, eh = dense_gate.shape[1], shared_gate.shape[1], expert_gate.shape[2]
    others = max(1, n_dp - 1)
    dma = pltpu.SemaphoreType.DMA
    vmem = pl.BlockSpec(memory_space=pltpu.VMEM)
    hbm = pl.BlockSpec(memory_space=pl.ANY)
    flops = 6 * width * rows * (ff + sh + n_dp * eh)
    moved = 6 * width * (ff + sh + eh)
    return pl.pallas_call(
        functools.partial(kernel, n_dp, n_mp),
        out_shape=jax.ShapeDtypeStruct((block, width), BF16),
        in_specs=[hbm, vmem, vmem] + [hbm] * 9 + [vmem, vmem],
        out_specs=vmem,
        scratch_shapes=[
            pltpu.VMEM((rows, width), BF16),
            pltpu.VMEM((width, ff), BF16),
            pltpu.VMEM((width, ff), BF16),
            pltpu.VMEM((ff, width), BF16),
            pltpu.VMEM((width, sh), BF16),
            pltpu.VMEM((width, sh), BF16),
            pltpu.VMEM((sh, width), BF16),
            pltpu.VMEM((width, eh), BF16),
            pltpu.VMEM((width, eh), BF16),
            pltpu.VMEM((eh, width), BF16),
            pltpu.VMEM((rows, ff), BF16),
            pltpu.VMEM((rows, sh), BF16),
            pltpu.VMEM((rows, eh), BF16),
            pltpu.VMEM((n_dp, rows, 128), F32),
            pltpu.VMEM((chips, CORES, block, width), BF16),
            pltpu.VMEM((n_dp, chips, CORES, block, width), BF16),
            pltpu.VMEM((chips, block, width), BF16),
            pltpu.VMEM((chips, block, width), BF16),
            pltpu.VMEM((n_dp, chips, block, width), BF16),
            pltpu.VMEM((others, chips, block, width), BF16),
            pltpu.VMEM((chips, block, width), BF16),
            dma((10,)),
            dma((others,)),
            dma((others,)),
            dma((CHUNKS,)),
            dma((CHUNKS,)),
            dma((chips,)),
            dma((chips,)),
            dma((chips,)),
            dma((chips,)),
            dma((n_dp, chips)),
            dma((n_dp, chips)),
            dma((others, chips)),
            dma((others, chips)),
            dma((n_dp, CHUNKS)),
            dma((n_dp, CHUNKS)),
            dma((others, chips)),
            dma((others, chips)),
            dma((chips,)),
            dma((chips,)),
        ],
        compiler_params=pltpu.CompilerParams(
            collective_id=0,
            has_side_effects=True,
            vmem_limit_bytes=63 * 1024 * 1024,
        ),
        cost_estimate=pl.CostEstimate(flops=flops, bytes_accessed=moved, transcendentals=0),
    )(
        tokens,
        domain_ids.reshape(rows, 1),
        domain_bias,
        dense_gate,
        dense_up,
        dense_down,
        shared_gate,
        shared_up,
        shared_down,
        expert_gate,
        expert_up,
        expert_down,
        expert_ids,
        route_weights,
    )


def solution(mesh):
    n_dp, n_mp = mesh.shape["dp"], mesh.shape["mp"]
    return jax.shard_map(
        functools.partial(body, n_dp, n_mp),
        mesh=mesh,
        in_specs=(
            P("dp", None),
            P("dp"),
            P(),
            P(None, "mp"),
            P(None, "mp"),
            P("mp", None),
            P(None, "mp"),
            P(None, "mp"),
            P("mp", None),
            P("mp", None, "dp"),
            P("mp", None, "dp"),
            P("mp", "dp", None),
            P("dp", None),
            P("dp", None),
        ),
        out_specs=P(("dp", "mp"), None),
        check_vma=False,
    )
```
